32 devices in a mesh: groups: 2 (over x), tensor: 16 (over z, y, core).
Axes of the slice: x: 2, y: 2, z: 4, core: 2. Of those that a mesh axis runs over, the one named last changes fastest.
Arguments:
- tokens: bfloat16 [256, 4096], P(('groups', 'tensor')), parts along dimension 0, may hold values from -6 to 6
- gate_weight: bfloat16 [8192, 14336], P('groups', 'tensor'), parts along dimension 0, may hold values from -0.09375 to 0.09375
- up_weight: bfloat16 [8192, 14336], P('groups', 'tensor'), parts along dimension 0, may hold values from -0.09375 to 0.09375
- down_weight: bfloat16 [28672, 4096], P(('groups', 'tensor')), parts along dimension 0, may hold values from -0.046875 to 0.046875
- gate_step: bfloat16 [256, 14336], P('groups', 'tensor'), parts along dimension 0, as said below
- up_step: bfloat16 [256, 14336], P('groups', 'tensor'), parts along dimension 0, as said below
- down_step: bfloat16 [896, 4096], P(('groups', 'tensor')), parts along dimension 0, as said below
Outputs:
- gate_grad: bfloat16 [8192, 14336], P('groups', 'tensor'), parts along dimension 0
- up_grad: bfloat16 [8192, 14336], P('groups', 'tensor'), parts along dimension 0
- down_grad: bfloat16 [28672, 4096], P(('groups', 'tensor')), parts along dimension 0
- gate_step_grad: float32 [256, 14336], P('groups', 'tensor'), parts along dimension 0
- up_step_grad: float32 [256, 14336], P('groups', 'tensor'), parts along dimension 0
- down_step_grad: float32 [896, 4096], P(('groups', 'tensor')), parts along dimension 0
The draws below stay inside these ranges and needn't reach their ends.
There are 2 independent parts, one for each index of `groups`. The reference program is written for one: setup_inputs(seed, part) draws one part's arguments, and reference() takes and returns one part's arrays. A program takes and returns all parts, laid end to end along the dimension named above; each array names one. Nothing has to cross between parts.
Inputs may be any that keep to these rules, and one draw needn't show every extreme that they name: `gate_step`: every step size is a power of two. `up_step`: every step size is a power of two. `down_step`: every step size is a power of two.
All inputs are finite; a program needn't handle non-finite values.
Results may differ from the reference program's by a relative error of at most 0.012.
Values may be sent and summed in bfloat16 or wider, within the bound.
A program may use at most 256 MiB of HBM per device.

```python
import math
import jax
import jax.numpy as jnp
from jax import lax

D = 4096
FF = 14336
GS = 32
TOKENS = 128


def step_powers(key, row_count, col_count, fan_width):
    base_scale = 2.0 ** (-math.floor(math.log2(fan_width) / 2))
    powers = jax.random.randint(key, (row_count, col_count), 1, 4)
    factor = jnp.where(powers == 1, 0.5, jnp.where(powers == 2, 0.25, 0.125)).astype(jnp.float32)
    return (factor * base_scale).astype(jnp.bfloat16)


def draw_gate_step(key, part):
    key = jax.random.fold_in(key, 11)
    return step_powers(key, D // GS, FF, D)


def draw_up_step(key, part):
    key = jax.random.fold_in(key, 23)
    return step_powers(key, D // GS, FF, D)


def draw_down_step(key, part):
    key = jax.random.fold_in(key, 37)
    return step_powers(key, FF // GS, D, FF)


def level_of(stream_key, dims, cuts, low, high):
    def one(dim, blocks):
        draws = jax.random.uniform(jax.random.fold_in(jax.random.fold_in(stream_key, 6), dim), (blocks,), jnp.float32, low / len(cuts), high / len(cuts))
        return jnp.repeat(jnp.exp(draws), dims[dim] // blocks).reshape((-1,) + (1,) * (len(dims) - dim - 1))

    factor_of = one(*cuts[0])
    for cut in cuts[1:]:
        factor_of = factor_of * one(*cut)
    return factor_of


def gaussian(rng, extent, scale, reach, pieces=(), dtype=jnp.bfloat16):
    values = jax.random.normal(rng, extent, jnp.float32) * scale
    if len(pieces) > 0:
        values = level_of(rng, extent, pieces, -0.22, 0.18) * values
    return jnp.clip(values, min=-reach, max=reach).astype(dtype)


def setup_inputs(seed: int = 0, part: int = 0) -> dict:
    key_list = jax.random.split(jax.random.key(seed), 8)
    part_splits = jax.random.split(jax.random.fold_in(key_list[7], part), 8)
    tokens = gaussian(part_splits[0], (TOKENS, D), 1.0, 6.0, ((0, 16),))
    gate_weight = gaussian(part_splits[1], (D, FF), D ** -0.5, 0.09375, ((1, 16),))
    up_weight = gaussian(part_splits[2], (D, FF), D ** -0.5, 0.09375, ((1, 16),))
    down_weight = gaussian(part_splits[3], (FF, D), FF ** -0.5, 0.046875, ((0, 16),))
    gate_step = draw_gate_step(jax.random.fold_in(jax.random.fold_in(key_list[7], part), 71), part)
    up_step = draw_up_step(jax.random.fold_in(jax.random.fold_in(key_list[7], part), 71), part)
    down_step = draw_down_step(jax.random.fold_in(jax.random.fold_in(key_list[7], part), 71), part)
    return {"tokens": tokens, "gate_weight": gate_weight, "up_weight": up_weight, "down_weight": down_weight, "gate_step": gate_step, "up_step": up_step, "down_step": down_step}


def fake_quant(weight, step_size):
    group_count, columns = step_size.shape
    step_wide = step_size.astype(jnp.float32)[:, None, :]
    scaled = weight.astype(jnp.float32).reshape(group_count, -1, columns) / step_wide
    levels = jnp.clip(jnp.floor(scaled + 0.5), -8.0, 7.0)
    inside = (scaled >= -8.0) & (scaled <= 7.0)
    fake_weight = (levels * step_wide).reshape(weight.shape).astype(jnp.bfloat16)
    step_slope = jnp.where(inside, levels - scaled, levels)
    return (fake_weight, inside, step_slope)

def latent_grads(full_grad, inside, step_slope):
    group_count = inside.shape[0]
    columns = inside.shape[2]
    shaped = full_grad.reshape(group_count, -1, columns)
    latent = jnp.where(inside, shaped, 0.0).reshape(full_grad.shape).astype(jnp.bfloat16)
    step_grad = lax.optimization_barrier(jnp.sum(shaped * step_slope, axis=1)) * (1.0 / math.sqrt(shaped.shape[1] * 7.0))
    return (latent, step_grad)

def reference(tokens, gate_weight, up_weight, down_weight, gate_step, up_step, down_step):
    gate_fake, gate_inside, gate_slope = fake_quant(gate_weight, gate_step)
    up_fake, up_inside, up_slope = fake_quant(up_weight, up_step)
    down_fake, down_inside, down_slope = fake_quant(down_weight, down_step)
    teacher_gate = jnp.dot(tokens, gate_weight, preferred_element_type=jnp.float32)
    teacher_up = jnp.dot(tokens, up_weight, preferred_element_type=jnp.float32)
    teacher_hidden = (jax.nn.silu(teacher_gate) * teacher_up).astype(jnp.bfloat16)
    teacher = jnp.dot(teacher_hidden, down_weight, preferred_element_type=jnp.float32)
    gate_pre = jnp.dot(tokens, gate_fake, preferred_element_type=jnp.float32)
    up_pre = jnp.dot(tokens, up_fake, preferred_element_type=jnp.float32)
    sigmoid_gate = jax.nn.sigmoid(gate_pre)
    silu_gate = gate_pre * sigmoid_gate
    hidden = (silu_gate * up_pre).astype(jnp.bfloat16)
    student = jnp.dot(hidden, down_fake, preferred_element_type=jnp.float32)
    error = (student - teacher).astype(jnp.bfloat16)
    down_full = lax.dot_general(hidden, error, (((0,), (0,)), ((), ())), preferred_element_type=jnp.float32)
    hidden_grad = lax.dot_general(error, down_fake, (((1,), (1,)), ((), ())), preferred_element_type=jnp.float32)
    gate_pre_grad = (hidden_grad * up_pre * sigmoid_gate * (1.0 + gate_pre * (1.0 - sigmoid_gate))).astype(jnp.bfloat16)
    up_pre_grad = (hidden_grad * silu_gate).astype(jnp.bfloat16)
    gate_full = lax.dot_general(tokens, gate_pre_grad, (((0,), (0,)), ((), ())), preferred_element_type=jnp.float32)
    up_full = lax.dot_general(tokens, up_pre_grad, (((0,), (0,)), ((), ())), preferred_element_type=jnp.float32)
    gate_grad, gate_step_grad = latent_grads(gate_full, gate_inside, gate_slope)
    up_grad, up_step_grad = latent_grads(up_full, up_inside, up_slope)
    down_grad, down_step_grad = latent_grads(down_full, down_inside, down_slope)
    return (gate_grad, up_grad, down_grad, gate_step_grad, up_step_grad, down_step_grad)
```

```python
import functools
import math

import jax
import jax.numpy as jnp
from jax import lax
from jax.experimental import pallas as pl
from jax.experimental.pallas import tpu as pltpu
from jax.sharding import PartitionSpec as P

F32 = jnp.float32
BF16 = jnp.bfloat16
MESH = pl.DeviceIdType.MESH
GROUP = 32
CHUNKS = 4
VMEM_LIMIT = 56 * 1024 * 1024


def place(Z, Y):
    me = lax.axis_index("tensor")
    core = lax.rem(me, 2)
    y = lax.rem(me // 2, Y)
    z = me // (2 * Y)
    return z, y, core


def meet(Z, Y, z, y, core):
    peers = [(lax.rem(z + d, Z) * Y + y) * 2 + core for d in range(1, Z)]
    peers.append((z * Y + (1 - y)) * 2 + core)
    peers.append((z * Y + y) * 2 + (1 - core))
    barrier = pltpu.get_barrier_semaphore()
    for peer in peers:
        pl.semaphore_signal(barrier, inc=1, device_id={"tensor": peer}, device_id_type=MESH)
    pl.semaphore_wait(barrier, len(peers))
    return peers


def remote(src, dst, send, recv, peer):
    return pltpu.make_async_remote_copy(
        src_ref=src, dst_ref=dst, send_sem=send, recv_sem=recv,
        device_id={"tensor": peer}, device_id_type=MESH,
    )


def spread_line(out, cols, sems, k, base, Z, z, y, core, peers):
    send, recv = sems
    copies = []
    for d in range(Z - 1):
        part = out.at[z, y, core, :, cols]
        copies.append(remote(part, part, send.at[k, base + d], recv.at[k, base + d], peers[d]))
        copies[-1].start()
    return copies


def spread_rest(out, chunks, line, sems, base, Z, z, y, core, peers):
    send, recv = sems
    rows, pair = [], []
    for k, cols in enumerate(chunks):
        for copy in line[k]:
            copy.wait_recv()
        part = out.at[:, y, core, :, cols]
        rows.append(remote(part, part, send.at[k, base], recv.at[k, base], peers[Z - 1]))
        rows[-1].start()
    for k, cols in enumerate(chunks):
        rows[k].wait_recv()
        part = out.at[:, :, core, :, cols]
        pair.append(remote(part, part, send.at[k, base + 1], recv.at[k, base + 1], peers[Z]))
        pair[-1].start()
    for k in range(len(chunks)):
        pair[k].wait_recv()
        for copy in line[k] + [rows[k], pair[k]]:
            copy.wait_send()


def gather_kernel(Z, Y, x_ref, out, send, recv):
    z, y, core = place(Z, Y)
    width = x_ref.shape[1] // CHUNKS
    chunks = [pl.ds(k * width, width) for k in range(CHUNKS)]
    out[z, y, core] = x_ref[...]
    peers = meet(Z, Y, z, y, core)
    line = [
        spread_line(out, cols, (send, recv), k, 0, Z, z, y, core, peers)
        for k, cols in enumerate(chunks)
    ]
    spread_rest(out, chunks, line, (send, recv), Z - 1, Z, z, y, core, peers)


def sum_gather_kernel(Z, Y, p_ref, out, from_core, to_y, mine, from_y, to_z, from_z, send, recv):
    z, y, core = place(Z, Y)
    width = p_ref.shape[-1] // CHUNKS
    chunks = [pl.ds(k * width, width) for k in range(CHUNKS)]
    peers = meet(Z, Y, z, y, core)
    waiting = []
    first = []
    for k, cols in enumerate(chunks):
        copy = remote(
            p_ref.at[:, :, 1 - core, :, cols], from_core.at[:, :, :, cols],
            send.at[k, 0], recv.at[k, 0], peers[Z],
        )
        copy.start()
        first.append(copy)
    second = []
    for k, cols in enumerate(chunks):
        first[k].wait_recv()
        for i in range(Z):
            to_y[i, :, cols] = (
                p_ref[i, 1 - y, core, :, cols].astype(F32)
                + from_core[i, 1 - y, :, cols].astype(F32)
            ).astype(BF16)
        copy = remote(
            to_y.at[:, :, cols], from_y.at[:, :, cols], send.at[k, 1], recv.at[k, 1], peers[Z - 1]
        )
        copy.start()
        second.append(copy)
        for i in range(Z):
            mine[i, :, cols] = (
                p_ref[i, y, core, :, cols].astype(F32) + from_core[i, y, :, cols].astype(F32)
            )
    third = []
    for k, cols in enumerate(chunks):
        second[k].wait_recv()
        for i in range(Z):
            mine[i, :, cols] = mine[i, :, cols] + from_y[i, :, cols].astype(F32)
        third.append([])
        for d in range(Z - 1):
            there = lax.rem(z + d + 1, Z)
            to_z[d, :, cols] = mine[there, :, cols].astype(BF16)
            copy = remote(
                to_z.at[d, :, cols], from_z.at[d, :, cols],
                send.at[k, 2 + d], recv.at[k, 2 + d], peers[d],
            )
            copy.start()
            third[k].append(copy)
    line = []
    for k, cols in enumerate(chunks):
        total = mine[z, :, cols]
        for d in range(Z - 1):
            third[k][d].wait_recv()
            total = total + from_z[d, :, cols].astype(F32)
        out[z, y, core, :, cols] = total.astype(BF16)
        line.append(spread_line(out, cols, (send, recv), k, Z + 1, Z, z, y, core, peers))
    spread_rest(out, chunks, line, (send, recv), 2 * Z, Z, z, y, core, peers)
    for k in range(CHUNKS):
        for copy in [first[k], second[k]] + third[k]:
            copy.wait_send()


def split_axis(count):
    return count // 4, 2


def gather_tokens(tokens, count):
    Z, Y = split_axis(count)
    rows, width = tokens.shape
    out = pl.pallas_call(
        functools.partial(gather_kernel, Z, Y),
        out_shape=jax.ShapeDtypeStruct((Z, Y, 2, rows, width), BF16),
        in_specs=[pl.BlockSpec(memory_space=pltpu.VMEM)],
        out_specs=pl.BlockSpec(memory_space=pltpu.VMEM),
        scratch_shapes=[
            pltpu.SemaphoreType.DMA((CHUNKS, Z + 1)),
            pltpu.SemaphoreType.DMA((CHUNKS, Z + 1)),
        ],
        compiler_params=pltpu.CompilerParams(
            collective_id=0, has_side_effects=True, vmem_limit_bytes=VMEM_LIMIT
        ),
        name="gather_tokens",
    )(tokens)
    return out.reshape(count * rows, width)


def sum_gather(partial, count):
    Z, Y = split_axis(count)
    width = partial.shape[1]
    rows = partial.shape[0] // count
    out = pl.pallas_call(
        functools.partial(sum_gather_kernel, Z, Y),
        out_shape=jax.ShapeDtypeStruct((Z, Y, 2, rows, width), BF16),
        in_specs=[pl.BlockSpec(memory_space=pltpu.VMEM)],
        out_specs=pl.BlockSpec(memory_space=pltpu.VMEM),
        scratch_shapes=[
            pltpu.VMEM((Z, Y, rows, width), BF16),
            pltpu.VMEM((Z, rows, width), BF16),
            pltpu.VMEM((Z, rows, width), F32),
            pltpu.VMEM((Z, rows, width), BF16),
            pltpu.VMEM((Z - 1, rows, width), BF16),
            pltpu.VMEM((Z - 1, rows, width), BF16),
            pltpu.SemaphoreType.DMA((CHUNKS, 2 * Z + 2)),
            pltpu.SemaphoreType.DMA((CHUNKS, 2 * Z + 2)),
        ],
        compiler_params=pltpu.CompilerParams(
            collective_id=1, has_side_effects=True, vmem_limit_bytes=VMEM_LIMIT
        ),
        name="sum_gather_error",
    )(partial.reshape(Z, Y, 2, rows, width))
    return out.reshape(partial.shape)


def prepare_steps(s_ref, s_scr, r_scr):
    steps = s_ref[...].astype(F32)
    s_scr[...] = steps
    r_scr[...] = 1.0 / steps


def quantize(w_ref, s_scr, r_scr, fake):
    for g in range(s_scr.shape[0]):
        rows = pl.ds(g * GROUP, GROUP)
        scaled = w_ref[rows, :].astype(F32) * r_scr[pl.ds(g, 1), :]
        levels = jnp.floor(jnp.clip(scaled, -8.0, 7.0) + 0.5)
        fake[rows, :] = (levels * s_scr[pl.ds(g, 1), :]).astype(BF16)


def latent(w_ref, s_scr, r_scr, full, grad_ref, step_ref, fake=None):
    factor = 1.0 / math.sqrt(GROUP * 7.0)
    for g in range(s_scr.shape[0]):
        rows = pl.ds(g * GROUP, GROUP)
        scaled = w_ref[rows, :].astype(F32) * r_scr[pl.ds(g, 1), :]
        clipped = jnp.clip(scaled, -8.0, 7.0)
        levels = jnp.floor(clipped + 0.5)
        inside = clipped == scaled
        if fake is not None:
            fake[rows, :] = (levels * s_scr[pl.ds(g, 1), :]).astype(BF16)
        part = full[rows, :]
        grad_ref[rows, :] = jnp.where(inside, part, 0.0).astype(BF16)
        slope = levels - jnp.where(inside, scaled, 0.0)
        step_ref[pl.ds(g, 1), :] = jnp.sum(part * slope, axis=0, keepdims=True) * factor


def dot(a, b):
    return jnp.dot(a, b, preferred_element_type=F32)


def forward_kernel(
    T, tok, gw, uw, dw, gs, us, ds,
    partial, gate_pre, up_pre, hidden,
    tg, tu, th, s_scr, r_scr, sd_scr, rd_scr, fake, fake_d,
):
    i = pl.program_id(0)

    @pl.when(i == 0)
    def _():
        for ref in (tg, tu, gate_pre, up_pre):
            ref[...] = jnp.zeros_like(ref)

    @pl.when(i < T)
    def _():
        x = tok[...]
        for w, s, teacher, pre in ((gw, gs, tg, gate_pre), (uw, us, tu, up_pre)):
            prepare_steps(s, s_scr, r_scr)
            quantize(w, s_scr, r_scr, fake)
            teacher[...] += dot(x, w[...])
            pre[...] += dot(x, fake[...])

    @pl.when(i == T - 1)
    def _():
        v = tg[...]
        th[...] = (v * jax.nn.sigmoid(v) * tu[...]).astype(BF16)
        v = gate_pre[...]
        hidden[...] = (v * jax.nn.sigmoid(v) * up_pre[...]).astype(BF16)

    @pl.when(i >= T)
    def _():
        prepare_steps(ds, sd_scr, rd_scr)
        quantize(dw, sd_scr, rd_scr, fake_d)
        partial[...] = (dot(hidden[...], fake_d[...]) - dot(th[...], dw[...])).astype(BF16)


def backward_kernel(
    T, err, tok, hidden, gate_pre, up_pre, gw, uw, dw, gs, us, ds,
    gg, ug, dg, gsg, usg, dsg,
    hidden_t, hg, gpg, upg, s_scr, r_scr, sd_scr, rd_scr, full, full_d, fake_d,
):
    i = pl.program_id(0)

    @pl.when(i == 0)
    def _():
        hidden_t[...] = hidden[...].T
        hg[...] = jnp.zeros_like(hg)

    @pl.when(i < T)
    def _():
        e = err[...]
        full_d[...] = dot(hidden_t[...], e)
        prepare_steps(ds, sd_scr, rd_scr)
        latent(dw, sd_scr, rd_scr, full_d, dg, dsg, fake_d)
        hg[...] += lax.dot_general(
            e, fake_d[...], (((1,), (1,)), ((), ())), preferred_element_type=F32
        )

    @pl.when(i == T)
    def _():
        v = gate_pre[...]
        sigma = jax.nn.sigmoid(v)
        h = hg[...]
        gpg[...] = (h * up_pre[...] * sigma * (1.0 + v * (1.0 - sigma))).astype(BF16)
        upg[...] = (h * (v * sigma)).astype(BF16)

    @pl.when(i >= T)
    def _():
        xt = tok[...].T
        for w, s, pg, grad, step in ((gw, gs, gpg, gg, gsg), (uw, us, upg, ug, usg)):
            full[...] = dot(xt, pg[...])
            prepare_steps(s, s_scr, r_scr)
            latent(w, s_scr, r_scr, full, grad, step)


def specs(T, tile, rows, ff, early):
    a = (lambda i: jnp.minimum(i, T - 1)) if early else (lambda i: jnp.maximum(i - T, 0))
    b = (lambda i: jnp.maximum(i - T, 0)) if early else (lambda i: jnp.minimum(i, T - 1))
    return {
        "tok": pl.BlockSpec((rows, tile), lambda i: (0, a(i))),
        "wide": pl.BlockSpec((tile, ff), lambda i: (a(i), 0)),
        "wide_step": pl.BlockSpec((tile // GROUP, ff), lambda i: (a(i), 0)),
        "down": pl.BlockSpec((ff, tile), lambda i: (0, b(i))),
        "down_step": pl.BlockSpec((ff // GROUP, tile), lambda i: (0, b(i))),
        "rows": pl.BlockSpec((rows, tile), lambda i: (0, b(i))),
        "whole": pl.BlockSpec((rows, ff), lambda i: (0, 0)),
    }


def step_scratch(tile, ff):
    return [
        pltpu.VMEM((tile // GROUP, ff), F32),
        pltpu.VMEM((tile // GROUP, ff), F32),
        pltpu.VMEM((ff // GROUP, tile), F32),
        pltpu.VMEM((ff // GROUP, tile), F32),
    ]


def body(tokens, gate_weight, up_weight, down_weight, gate_step, up_step, down_step, *, count):
    D, ff = gate_weight.shape
    tile = 512
    T = D // tile
    whole = gather_tokens(tokens, count)
    rows = whole.shape[0]
    shape = jax.ShapeDtypeStruct
    params = pltpu.CompilerParams(
        dimension_semantics=("arbitrary",), vmem_limit_bytes=VMEM_LIMIT
    )
    b = specs(T, tile, rows, ff, True)
    partial, gate_pre, up_pre, hidden = pl.pallas_call(
        functools.partial(forward_kernel, T),
        grid=(2 * T,),
        in_specs=[b["tok"], b["wide"], b["wide"], b["down"],
                  b["wide_step"], b["wide_step"], b["down_step"]],
        out_specs=[b["rows"], b["whole"], b["whole"], b["whole"]],
        out_shape=[shape((rows, D), BF16), shape((rows, ff), F32),
                   shape((rows, ff), F32), shape((rows, ff), BF16)],
        scratch_shapes=[
            pltpu.VMEM((rows, ff), F32), pltpu.VMEM((rows, ff), F32), pltpu.VMEM((rows, ff), BF16),
            *step_scratch(tile, ff),
            pltpu.VMEM((tile, ff), BF16), pltpu.VMEM((ff, tile), BF16),
        ],
        compiler_params=params,
        name="forward",
    )(whole, gate_weight, up_weight, down_weight, gate_step, up_step, down_step)
    error = sum_gather(partial, count)
    b = specs(T, tile, rows, ff, False)
    return tuple(pl.pallas_call(
        functools.partial(backward_kernel, T),
        grid=(2 * T,),
        in_specs=[b["rows"], b["tok"], b["whole"], b["whole"], b["whole"],
                  b["wide"], b["wide"], b["down"],
                  b["wide_step"], b["wide_step"], b["down_step"]],
        out_specs=[b["wide"], b["wide"], b["down"],
                   b["wide_step"], b["wide_step"], b["down_step"]],
        out_shape=[shape((D, ff), BF16), shape((D, ff), BF16), shape((ff, D), BF16),
                   shape(gate_step.shape, F32), shape(up_step.shape, F32),
                   shape(down_step.shape, F32)],
        scratch_shapes=[
            pltpu.VMEM((ff, rows), BF16), pltpu.VMEM((rows, ff), F32),
            pltpu.VMEM((rows, ff), BF16), pltpu.VMEM((rows, ff), BF16),
            *step_scratch(tile, ff),
            pltpu.VMEM((tile, ff), F32), pltpu.VMEM((ff, tile), F32), pltpu.VMEM((ff, tile), BF16),
        ],
        compiler_params=params,
        name="backward",
    )(error, whole, hidden, gate_pre, up_pre, gate_weight, up_weight, down_weight,
      gate_step, up_step, down_step))


def solution(mesh):
    return jax.shard_map(
        functools.partial(body, count=mesh.shape["tensor"]),
        mesh=mesh,
        in_specs=(
            P(("groups", "tensor"), None),
            P("groups", "tensor"),
            P("groups", "tensor"),
            P(("groups", "tensor"), None),
            P("groups", "tensor"),
            P("groups", "tensor"),
            P(("groups", "tensor"), None),
        ),
        out_specs=(
            P("groups", "tensor"),
            P("groups", "tensor"),
            P(("groups", "tensor"), None),
            P("groups", "tensor"),
            P("groups", "tensor"),
            P(("groups", "tensor"), None),
        ),
        check_vma=False,
    )
```

```python
import functools
import math

import jax
import jax.numpy as jnp
from jax import lax
from jax.experimental import pallas as pl
from jax.experimental.pallas import tpu as pltpu
from jax.sharding import PartitionSpec as P

F32 = jnp.float32
BF16 = jnp.bfloat16
MESH = pl.DeviceIdType.MESH
GROUP = 32
CHUNKS = 4
VMEM_LIMIT = 56 * 1024 * 1024


def place(Z, Y):
    me = lax.axis_index("tensor")
    core = lax.rem(me, 2)
    y = lax.rem(me // 2, Y)
    z = me // (2 * Y)
    return z, y, core


def meet(Z, Y, z, y, core):
    peers = [(lax.rem(z + d, Z) * Y + y) * 2 + core for d in range(1, Z)]
    peers.append((z * Y + (1 - y)) * 2 + core)
    peers.append((z * Y + y) * 2 + (1 - core))
    barrier = pltpu.get_barrier_semaphore()
    for peer in peers:
        pl.semaphore_signal(barrier, inc=1, device_id={"tensor": peer}, device_id_type=MESH)
    pl.semaphore_wait(barrier, len(peers))
    return peers


def remote(src, dst, send, recv, peer):
    return pltpu.make_async_remote_copy(
        src_ref=src, dst_ref=dst, send_sem=send, recv_sem=recv,
        device_id={"tensor": peer}, device_id_type=MESH,
    )


def spread_line(out, cols, sems, k, base, Z, z, y, core, peers):
    send, recv = sems
    copies = []
    for d in range(Z - 1):
        part = out.at[z, y, core, :, cols]
        copies.append(remote(part, part, send.at[k, base + d], recv.at[k, base + d], peers[d]))
        copies[-1].start()
    return copies


def spread_rest(out, chunks, line, sems, base, Z, z, y, core, peers, work):
    send, recv = sems
    rows, pair = [], []
    for k, cols in enumerate(chunks):
        work()
        for copy in line[k]:
            copy.wait_recv()
        part = out.at[:, y, core, :, cols]
        rows.append(remote(part, part, send.at[k, base], recv.at[k, base], peers[Z - 1]))
        rows[-1].start()
    for k, cols in enumerate(chunks):
        work()
        rows[k].wait_recv()
        part = out.at[:, :, core, :, cols]
        pair.append(remote(part, part, send.at[k, base + 1], recv.at[k, base + 1], peers[Z]))
        pair[-1].start()
    for k in range(len(chunks)):
        work()
        pair[k].wait_recv()
    return rows + pair


def split_axis(count):
    return count // 4, 2


def quantize(w_ref, s_scr, base, groups, fake):
    @pl.loop(0, groups)
    def _(g):
        rows = pl.ds(pl.multiple_of(g * GROUP, GROUP), GROUP)
        step = s_scr[pl.ds(base + g, 1), :]
        scaled = w_ref[rows, :].astype(F32) * (1.0 / step)
        levels = jnp.floor(jnp.clip(scaled, -8.0, 7.0) + 0.5)
        fake[rows, :] = (levels * step).astype(BF16)


def slope_in_place(w_ref, s_scr, base, groups):
    @pl.loop(0, groups)
    def _(g):
        rows = pl.ds(pl.multiple_of(g * GROUP, GROUP), GROUP)
        scaled = w_ref[rows, :].astype(F32) * (1.0 / s_scr[pl.ds(base + g, 1), :])
        clipped = jnp.clip(scaled, -8.0, 7.0)
        levels = jnp.floor(clipped + 0.5)
        slope = levels - jnp.where(clipped == scaled, scaled, 0.0)
        w_ref[rows, :] = slope.astype(BF16)


def latent(slope_ref, full, grad_ref, step_ref):
    factor = 1.0 / math.sqrt(GROUP * 7.0)
    for g in range(step_ref.shape[0]):
        rows = pl.ds(g * GROUP, GROUP)
        slope = slope_ref[rows, :].astype(F32)
        part = full[rows, :]
        grad_ref[rows, :] = jnp.where(jnp.abs(slope) <= 0.5, part, 0.0).astype(BF16)
        step_ref[pl.ds(g, 1), :] = jnp.sum(part * slope, axis=0, keepdims=True) * factor


def dot(a, b):
    return jnp.dot(a, b, preferred_element_type=F32)


def front_kernel(
    Z, Y, T, x_ref, gw, uw, dw, gs, us, ds,
    out_x, out, gate_pre, up_pre, hidden, slope_g, slope_u, slope_d, out_fd,
    w_g, w_u, w_d, f_g, f_u, f_d, s_g, s_u, s_d, x2d, tg, tu, th,
    p_ref, from_core, to_y, mine, from_y, to_z, from_z,
    in_sem, out_sem, send0, recv0, send, recv,
):
    z, y, core = place(Z, Y)
    D, ff = gw.shape
    rows = x2d.shape[1]
    tile = D // T
    wide = [pl.ds(t * tile, tile) for t in range(T)]
    width = D // CHUNKS
    chunks = [pl.ds(k * width, width) for k in range(CHUNKS)]

    loads = {}
    for t in range(T):
        loads["d", t] = pltpu.make_async_copy(dw.at[:, wide[t]], w_d.at[t], in_sem.at[2, t])
        loads["g", t] = pltpu.make_async_copy(gw.at[wide[t], :], w_g.at[t], in_sem.at[0, t])
        loads["u", t] = pltpu.make_async_copy(uw.at[wide[t], :], w_u.at[t], in_sem.at[1, t])
    order = [("d", t) for t in range(T)] + [(n, t) for t in range(T) for n in "gu"]
    for key in order:
        loads[key].start()
    out_x[z, y, core] = x_ref[...]
    peers = meet(Z, Y, z, y, core)
    line = [
        spread_line(out_x, cols, (send0, recv0), k, 0, Z, z, y, core, peers)
        for k, cols in enumerate(chunks)
    ]
    s_g[...] = gs[...].astype(F32)
    s_u[...] = us[...].astype(F32)
    for t in range(T):
        s_d[t] = ds[:, wide[t]].astype(F32)

    weights = {"g": (w_g, f_g, s_g, slope_g), "u": (w_u, f_u, s_u, slope_u),
               "d": (w_d, f_d, s_d, slope_d)}
    stores = []

    def pick(name, t):
        w, f, s, target = weights[name]
        if name == "d":
            return w.at[t], f.at[t], s.at[t], 0, ff // GROUP, target.at[:, wide[t]]
        return w.at[t], f.at[t], s, t * (tile // GROUP), tile // GROUP, target.at[wide[t], :]

    def quantize_one(key):
        loads[key].wait()
        w, f, s, base, groups, _ = pick(*key)
        quantize(w, s, base, groups, f)
        if key[0] == "d":
            copy = pltpu.make_async_copy(f, out_fd.at[:, wide[key[1]]], out_sem.at[3, key[1]])
            copy.start()
            stores.append(copy)

    def slope_one(key):
        w, _, s, base, groups, target = pick(*key)
        slope_in_place(w, s, base, groups)
        copy = pltpu.make_async_copy(w, target, out_sem.at["gud".index(key[0]), key[1]])
        copy.start()
        stores.append(copy)

    def worker(do, each):
        left = list(order)

        def work(count=each):
            for key in left[:count]:
                do(key)
            del left[:count]

        return work

    work = worker(quantize_one, 2)
    ends = [spread_rest(out_x, chunks, line, (send0, recv0), Z - 1, Z, z, y, core, peers, work)]
    ends += line
    work(3 * T)

    for t in range(T):
        x2d[t] = out_x[:, :, :, :, wide[t]].astype(F32).reshape(rows, tile).astype(BF16)
    for ref in (tg, tu, gate_pre, up_pre):
        ref[...] = jnp.zeros_like(ref)

    @pl.loop(0, T)
    def _(t):
        x = x2d[t]
        tg[...] += dot(x, w_g[t])
        tu[...] += dot(x, w_u[t])
        gate_pre[...] += dot(x, f_g[t])
        up_pre[...] += dot(x, f_u[t])

    v = tg[...]
    th[...] = (v * jax.nn.sigmoid(v) * tu[...]).astype(BF16)
    v = gate_pre[...]
    hidden[...] = (v * jax.nn.sigmoid(v) * up_pre[...]).astype(BF16)

    first = []
    per = T // CHUNKS
    for k, cols in enumerate(chunks):
        for t in range(k * per, (k + 1) * per):
            part = dot(hidden[...], f_d[t]) - dot(th[...], w_d[t])
            p_ref[:, :, :, :, wide[t]] = part.reshape(Z, Y, 2, rows // (4 * Z), tile).astype(BF16)
        copy = remote(
            p_ref.at[:, :, 1 - core, :, cols], from_core.at[:, :, :, cols],
            send.at[k, 0], recv.at[k, 0], peers[Z],
        )
        copy.start()
        first.append(copy)

    work = worker(slope_one, 1)
    second = []
    for k, cols in enumerate(chunks):
        first[k].wait_recv()
        for i in range(Z):
            to_y[i, :, cols] = (
                p_ref[i, 1 - y, core, :, cols].astype(F32)
                + from_core[i, 1 - y, :, cols].astype(F32)
            ).astype(BF16)
        copy = remote(
            to_y.at[:, :, cols], from_y.at[:, :, cols], send.at[k, 1], recv.at[k, 1], peers[Z - 1]
        )
        copy.start()
        second.append(copy)
        for i in range(Z):
            mine[i, :, cols] = (
                p_ref[i, y, core, :, cols].astype(F32) + from_core[i, y, :, cols].astype(F32)
            )
    third = []
    for k, cols in enumerate(chunks):
        work()
        second[k].wait_recv()
        for i in range(Z):
            mine[i, :, cols] = mine[i, :, cols] + from_y[i, :, cols].astype(F32)
        third.append([])
        for d in range(Z - 1):
            there = lax.rem(z + d + 1, Z)
            to_z[d, :, cols] = mine[there, :, cols].astype(BF16)
            copy = remote(
                to_z.at[d, :, cols], from_z.at[d, :, cols],
                send.at[k, 2 + d], recv.at[k, 2 + d], peers[d],
            )
            copy.start()
            third[k].append(copy)
    line = []
    for k, cols in enumerate(chunks):
        work()
        total = mine[z, :, cols]
        for d in range(Z - 1):
            third[k][d].wait_recv()
            total = total + from_z[d, :, cols].astype(F32)
        out[z, y, core, :, cols] = total.astype(BF16)
        line.append(spread_line(out, cols, (send, recv), k, Z + 1, Z, z, y, core, peers))
    ends.append(spread_rest(out, chunks, line, (send, recv), 2 * Z, Z, z, y, core, peers, work))
    work(3 * T)
    ends += line + third + [first, second, stores]
    for group in ends:
        for copy in group:
            if group is stores:
                copy.wait()
            else:
                copy.wait_send()


def backward_kernel(
    T, err, tok, hidden, gate_pre, up_pre, gl, ul, dl, fd,
    gg, ug, dg, gsg, usg, dsg,
    hidden_t, hg, gpg, upg, full, full_d,
):
    i = pl.program_id(0)

    @pl.when(i == 0)
    def _():
        hidden_t[...] = hidden[...].T
        hg[...] = jnp.zeros_like(hg)

    @pl.when(i < T)
    def _():
        e = err[...]
        full_d[...] = dot(hidden_t[...], e)
        hg[...] += lax.dot_general(
            e, fd[...], (((1,), (1,)), ((), ())), preferred_element_type=F32
        )
        latent(dl, full_d, dg, dsg)

    @pl.when(i == T)
    def _():
        v = gate_pre[...]
        sigma = jax.nn.sigmoid(v)
        h = hg[...]
        gpg[...] = (h * up_pre[...] * sigma * (1.0 + v * (1.0 - sigma))).astype(BF16)
        upg[...] = (h * (v * sigma)).astype(BF16)

    @pl.when(i >= T)
    def _():
        xt = tok[...].T
        for sl, pg, grad, step in ((gl, gpg, gg, gsg), (ul, upg, ug, usg)):
            full[...] = dot(xt, pg[...])
            latent(sl, full, grad, step)


def specs(T, tile, rows, ff, early):
    a = (lambda i: jnp.minimum(i, T - 1)) if early else (lambda i: jnp.maximum(i - T, 0))
    b = (lambda i: jnp.maximum(i - T, 0)) if early else (lambda i: jnp.minimum(i, T - 1))
    return {
        "tok": pl.BlockSpec((rows, tile), lambda i: (0, a(i))),
        "wide": pl.BlockSpec((tile, ff), lambda i: (a(i), 0)),
        "wide_step": pl.BlockSpec((tile // GROUP, ff), lambda i: (a(i), 0)),
        "down": pl.BlockSpec((ff, tile), lambda i: (0, b(i))),
        "down_step": pl.BlockSpec((ff // GROUP, tile), lambda i: (0, b(i))),
        "rows": pl.BlockSpec((rows, tile), lambda i: (0, b(i))),
        "whole": pl.BlockSpec((rows, ff), lambda i: (0, 0)),
    }


def body(tokens, gate_weight, up_weight, down_weight, gate_step, up_step, down_step, *, count):
    D, ff = gate_weight.shape
    tile = 512
    T = D // tile
    Z, Y = split_axis(count)
    part = tokens.shape[0]
    rows = part * count
    shape = jax.ShapeDtypeStruct
    vmem = pl.BlockSpec(memory_space=pltpu.VMEM)
    hbm = pl.BlockSpec(memory_space=pl.ANY)
    whole, error, gate_pre, up_pre, hidden, slope_g, slope_u, slope_d, fake_d = pl.pallas_call(
        functools.partial(front_kernel, Z, Y, T),
        in_specs=[vmem, hbm, hbm, hbm, vmem, vmem, vmem],
        out_specs=[vmem] * 5 + [hbm] * 4,
        out_shape=[
            shape((Z, Y, 2, part, D), BF16), shape((Z, Y, 2, part, D), BF16),
            shape((rows, ff), F32), shape((rows, ff), F32), shape((rows, ff), BF16),
            shape((D, ff), BF16), shape((D, ff), BF16), shape((ff, D), BF16), shape((ff, D), BF16),
        ],
        scratch_shapes=[
            pltpu.VMEM((T, tile, ff), BF16), pltpu.VMEM((T, tile, ff), BF16),
            pltpu.VMEM((T, ff, tile), BF16),
            pltpu.VMEM((T, tile, ff), BF16), pltpu.VMEM((T, tile, ff), BF16),
            pltpu.VMEM((T, ff, tile), BF16),
            pltpu.VMEM((D // GROUP, ff), F32), pltpu.VMEM((D // GROUP, ff), F32),
            pltpu.VMEM((T, ff // GROUP, tile), F32),
            pltpu.VMEM((T, rows, tile), BF16),
            pltpu.VMEM((rows, ff), F32), pltpu.VMEM((rows, ff), F32), pltpu.VMEM((rows, ff), BF16),
            pltpu.VMEM((Z, Y, 2, part, D), BF16),
            pltpu.VMEM((Z, Y, part, D), BF16),
            pltpu.VMEM((Z, part, D), BF16),
            pltpu.VMEM((Z, part, D), F32),
            pltpu.VMEM((Z, part, D), BF16),
            pltpu.VMEM((Z - 1, part, D), BF16),
            pltpu.VMEM((Z - 1, part, D), BF16),
            pltpu.SemaphoreType.DMA((3, T)),
            pltpu.SemaphoreType.DMA((4, T)),
            pltpu.SemaphoreType.DMA((CHUNKS, Z + 1)),
            pltpu.SemaphoreType.DMA((CHUNKS, Z + 1)),
            pltpu.SemaphoreType.DMA((CHUNKS, 2 * Z + 2)),
            pltpu.SemaphoreType.DMA((CHUNKS, 2 * Z + 2)),
        ],
        compiler_params=pltpu.CompilerParams(
            collective_id=0, has_side_effects=True, vmem_limit_bytes=60 * 1024 * 1024
        ),
        name="front",
    )(tokens, gate_weight, up_weight, down_weight, gate_step, up_step, down_step)
    whole = whole.reshape(rows, D)
    error = error.reshape(rows, D)
    b = specs(T, tile, rows, ff, False)
    return tuple(pl.pallas_call(
        functools.partial(backward_kernel, T),
        grid=(2 * T,),
        in_specs=[b["rows"], b["tok"], b["whole"], b["whole"], b["whole"],
                  b["wide"], b["wide"], b["down"], b["down"]],
        out_specs=[b["wide"], b["wide"], b["down"],
                   b["wide_step"], b["wide_step"], b["down_step"]],
        out_shape=[shape((D, ff), BF16), shape((D, ff), BF16), shape((ff, D), BF16),
                   shape(gate_step.shape, F32), shape(up_step.shape, F32),
                   shape(down_step.shape, F32)],
        scratch_shapes=[
            pltpu.VMEM((ff, rows), BF16), pltpu.VMEM((rows, ff), F32),
            pltpu.VMEM((rows, ff), BF16), pltpu.VMEM((rows, ff), BF16),
            pltpu.VMEM((tile, ff), F32), pltpu.VMEM((ff, tile), F32),
        ],
        compiler_params=pltpu.CompilerParams(
            dimension_semantics=("arbitrary",), vmem_limit_bytes=VMEM_LIMIT
        ),
        name="backward",
    )(error, whole, hidden, gate_pre, up_pre, slope_g, slope_u, slope_d, fake_d))


def solution(mesh):
    return jax.shard_map(
        functools.partial(body, count=mesh.shape["tensor"]),
        mesh=mesh,
        in_specs=(
            P(("groups", "tensor"), None),
            P("groups", "tensor"),
            P("groups", "tensor"),
            P(("groups", "tensor"), None),
            P("groups", "tensor"),
            P("groups", "tensor"),
            P(("groups", "tensor"), None),
        ),
        out_specs=(
            P("groups", "tensor"),
            P("groups", "tensor"),
            P(("groups", "tensor"), None),
            P("groups", "tensor"),
            P("groups", "tensor"),
            P(("groups", "tensor"), None),
        ),
        check_vma=False,
    )
```

```python
import functools
import math

import jax
import jax.numpy as jnp
from jax import lax
from jax.experimental import pallas as pl
from jax.experimental.pallas import tpu as pltpu
from jax.sharding import PartitionSpec as P

F32 = jnp.float32
BF16 = jnp.bfloat16
MESH = pl.DeviceIdType.MESH
GROUP = 32
CHUNKS = 4
VMEM_LIMIT = 56 * 1024 * 1024


def place(Z, Y):
    me = lax.axis_index("tensor")
    core = lax.rem(me, 2)
    y = lax.rem(me // 2, Y)
    z = me // (2 * Y)
    return z, y, core


def meet(Z, Y, z, y, core):
    peers = [(lax.rem(z + d, Z) * Y + y) * 2 + core for d in range(1, Z)]
    peers.append((z * Y + (1 - y)) * 2 + core)
    peers.append((z * Y + y) * 2 + (1 - core))
    barrier = pltpu.get_barrier_semaphore()
    for peer in peers:
        pl.semaphore_signal(barrier, inc=1, device_id={"tensor": peer}, device_id_type=MESH)
    pl.semaphore_wait(barrier, len(peers))
    return peers


def remote(src, dst, send, recv, peer):
    return pltpu.make_async_remote_copy(
        src_ref=src, dst_ref=dst, send_sem=send, recv_sem=recv,
        device_id={"tensor": peer}, device_id_type=MESH,
    )


def spread_line(out, cols, sems, k, base, Z, z, y, core, peers):
    send, recv = sems
    copies = []
    for d in range(Z - 1):
        part = out.at[z, y, core, :, cols]
        copies.append(remote(part, part, send.at[k, base + d], recv.at[k, base + d], peers[d]))
        copies[-1].start()
    return copies


def spread_rest(out, chunks, line, sems, base, Z, z, y, core, peers, work):
    send, recv = sems
    rows, pair = [], []
    for k, cols in enumerate(chunks):
        work()
        for copy in line[k]:
            copy.wait_recv()
        part = out.at[:, y, core, :, cols]
        rows.append(remote(part, part, send.at[k, base], recv.at[k, base], peers[Z - 1]))
        rows[-1].start()
    for k, cols in enumerate(chunks):
        work()
        rows[k].wait_recv()
        part = out.at[:, :, core, :, cols]
        pair.append(remote(part, part, send.at[k, base + 1], recv.at[k, base + 1], peers[Z]))
        pair[-1].start()
    for k in range(len(chunks)):
        work()
        pair[k].wait_recv()
    return rows + pair


def split_axis(count):
    return count // 4, 2


def quantize(w_ref, s_scr, base, groups, fake):
    @pl.loop(0, groups, unroll=4)
    def _(g):
        rows = pl.ds(pl.multiple_of(g * GROUP, GROUP), GROUP)
        step = s_scr[pl.ds(base + g, 1), :]
        scaled = w_ref[rows, :].astype(F32) * (1.0 / step)
        levels = jnp.floor(jnp.clip(scaled, -8.0, 7.0) + 0.5)
        fake[rows, :] = (levels * step).astype(BF16)


def slope_in_place(w_ref, s_scr, base, groups):
    @pl.loop(0, groups, unroll=4)
    def _(g):
        rows = pl.ds(pl.multiple_of(g * GROUP, GROUP), GROUP)
        scaled = w_ref[rows, :].astype(F32) * (1.0 / s_scr[pl.ds(base + g, 1), :])
        clipped = jnp.clip(scaled, -8.0, 7.0)
        levels = jnp.floor(clipped + 0.5)
        slope = levels - jnp.where(clipped == scaled, scaled, 0.0)
        w_ref[rows, :] = slope.astype(BF16)


def latent(slope_ref, full, grad_ref, step_ref):
    factor = 1.0 / math.sqrt(GROUP * 7.0)
    for g in range(step_ref.shape[0]):
        rows = pl.ds(g * GROUP, GROUP)
        slope = slope_ref[rows, :].astype(F32)
        part = full[rows, :]
        grad_ref[rows, :] = jnp.where(jnp.abs(slope) <= 0.5, part, 0.0).astype(BF16)
        step_ref[pl.ds(g, 1), :] = jnp.sum(part * slope, axis=0, keepdims=True) * factor


def dot(a, b):
    return jnp.dot(a, b, preferred_element_type=F32)


def front_kernel(
    Z, Y, T, x_ref, gw, uw, dw, gs, us, ds,
    out_x, out, gate_pre, up_pre, hidden, slope_g, slope_u, slope_d, out_fd,
    w_g, w_u, w_d, f_g, f_u, f_d, s_g, s_u, s_d, x2d, tg, tu, th,
    p_ref, from_core, to_y, mine, from_y, to_z, from_z,
    in_sem, out_sem, send0, recv0, send, recv,
):
    z, y, core = place(Z, Y)
    D, ff = gw.shape
    rows = x2d.shape[1]
    tile = D // T
    wide = [pl.ds(t * tile, tile) for t in range(T)]
    width = D // CHUNKS
    chunks = [pl.ds(k * width, width) for k in range(CHUNKS)]

    loads = {}
    for t in range(T):
        loads["d", t] = pltpu.make_async_copy(dw.at[:, wide[t]], w_d.at[t], in_sem.at[2, t])
        loads["g", t] = pltpu.make_async_copy(gw.at[wide[t], :], w_g.at[t], in_sem.at[0, t])
        loads["u", t] = pltpu.make_async_copy(uw.at[wide[t], :], w_u.at[t], in_sem.at[1, t])
    order = [("d", t) for t in range(T)] + [(n, t) for t in range(T) for n in "gu"]
    for key in order:
        loads[key].start()
    out_x[z, y, core] = x_ref[...]
    peers = meet(Z, Y, z, y, core)
    line = [
        spread_line(out_x, cols, (send0, recv0), k, 0, Z, z, y, core, peers)
        for k, cols in enumerate(chunks)
    ]
    s_g[...] = gs[...].astype(F32)
    s_u[...] = us[...].astype(F32)
    for t in range(T):
        s_d[t] = ds[:, wide[t]].astype(F32)

    weights = {"g": (w_g, f_g, s_g, slope_g), "u": (w_u, f_u, s_u, slope_u),
               "d": (w_d, f_d, s_d, slope_d)}
    stores = []

    def pick(name, t):
        w, f, s, target = weights[name]
        if name == "d":
            return w.at[t], f.at[t], s.at[t], 0, ff // GROUP, target.at[:, wide[t]]
        return w.at[t], f.at[t], s, t * (tile // GROUP), tile // GROUP, target.at[wide[t], :]

    def quantize_one(key):
        loads[key].wait()
        w, f, s, base, groups, _ = pick(*key)
        quantize(w, s, base, groups, f)
        if key[0] == "d":
            copy = pltpu.make_async_copy(f, out_fd.at[:, wide[key[1]]], out_sem.at[3, key[1]])
            copy.start()
            stores.append(copy)

    def slope_one(key):
        w, _, s, base, groups, target = pick(*key)
        slope_in_place(w, s, base, groups)
        copy = pltpu.make_async_copy(w, target, out_sem.at["gud".index(key[0]), key[1]])
        copy.start()
        stores.append(copy)

    def worker(do, each):
        left = list(order)

        def work(count=each):
            for key in left[:count]:
                do(key)
            del left[:count]

        return work

    work = worker(quantize_one, 2)
    ends = [spread_rest(out_x, chunks, line, (send0, recv0), Z - 1, Z, z, y, core, peers, work)]
    ends += line
    work(3 * T)

    for t in range(T):
        x2d[t] = out_x[:, :, :, :, wide[t]].astype(F32).reshape(rows, tile).astype(BF16)
    for ref in (tg, tu, gate_pre, up_pre):
        ref[...] = jnp.zeros_like(ref)

    @pl.loop(0, T)
    def _(t):
        x = x2d[t]
        tg[...] += dot(x, w_g[t])
        tu[...] += dot(x, w_u[t])
        gate_pre[...] += dot(x, f_g[t])
        up_pre[...] += dot(x, f_u[t])

    v = tg[...]
    th[...] = (v * jax.nn.sigmoid(v) * tu[...]).astype(BF16)
    v = gate_pre[...]
    hidden[...] = (v * jax.nn.sigmoid(v) * up_pre[...]).astype(BF16)

    first = []
    per = T // CHUNKS
    for k, cols in enumerate(chunks):
        for t in range(k * per, (k + 1) * per):
            part = dot(hidden[...], f_d[t]) - dot(th[...], w_d[t])
            p_ref[:, :, :, :, wide[t]] = part.reshape(Z, Y, 2, rows // (4 * Z), tile).astype(BF16)
        copy = remote(
            p_ref.at[:, :, 1 - core, :, cols], from_core.at[:, :, :, cols],
            send.at[k, 0], recv.at[k, 0], peers[Z],
        )
        copy.start()
        first.append(copy)

    work = worker(slope_one, 1)
    second = []
    for k, cols in enumerate(chunks):
        first[k].wait_recv()
        for i in range(Z):
            to_y[i, :, cols] = (
                p_ref[i, 1 - y, core, :, cols].astype(F32)
                + from_core[i, 1 - y, :, cols].astype(F32)
            ).astype(BF16)
        copy = remote(
            to_y.at[:, :, cols], from_y.at[:, :, cols], send.at[k, 1], recv.at[k, 1], peers[Z - 1]
        )
        copy.start()
        second.append(copy)
        for i in range(Z):
            mine[i, :, cols] = (
                p_ref[i, y, core, :, cols].astype(F32) + from_core[i, y, :, cols].astype(F32)
            )
    third = []
    for k, cols in enumerate(chunks):
        work()
        second[k].wait_recv()
        for i in range(Z):
            mine[i, :, cols] = mine[i, :, cols] + from_y[i, :, cols].astype(F32)
        third.append([])
        for d in range(Z - 1):
            there = lax.rem(z + d + 1, Z)
            to_z[d, :, cols] = mine[there, :, cols].astype(BF16)
            copy = remote(
                to_z.at[d, :, cols], from_z.at[d, :, cols],
                send.at[k, 2 + d], recv.at[k, 2 + d], peers[d],
            )
            copy.start()
            third[k].append(copy)
    line = []
    for k, cols in enumerate(chunks):
        work()
        total = mine[z, :, cols]
        for d in range(Z - 1):
            third[k][d].wait_recv()
            total = total + from_z[d, :, cols].astype(F32)
        out[z, y, core, :, cols] = total.astype(BF16)
        line.append(spread_line(out, cols, (send, recv), k, Z + 1, Z, z, y, core, peers))
    ends.append(spread_rest(out, chunks, line, (send, recv), 2 * Z, Z, z, y, core, peers, work))
    work(3 * T)
    ends += line + third + [first, second, stores]
    for group in ends:
        for copy in group:
            if group is stores:
                copy.wait()
            else:
                copy.wait_send()


def backward_kernel(
    T, err, tok, hidden, gate_pre, up_pre, gl, ul, dl, fd,
    gg, ug, dg, gsg, usg, dsg,
    hidden_t, hg, gpg, upg, full, full_d,
):
    i = pl.program_id(0)

    @pl.when(i == 0)
    def _():
        hidden_t[...] = hidden[...].T
        hg[...] = jnp.zeros_like(hg)

    @pl.when(i < T)
    def _():
        e = err[...]
        full_d[...] = dot(hidden_t[...], e)
        hg[...] += lax.dot_general(
            e, fd[...], (((1,), (1,)), ((), ())), preferred_element_type=F32
        )
        latent(dl, full_d, dg, dsg)

    @pl.when(i == T)
    def _():
        v = gate_pre[...]
        sigma = jax.nn.sigmoid(v)
        h = hg[...]
        gpg[...] = (h * up_pre[...] * sigma * (1.0 + v * (1.0 - sigma))).astype(BF16)
        upg[...] = (h * (v * sigma)).astype(BF16)

    @pl.when(i >= T)
    def _():
        xt = tok[...].T
        for sl, pg, grad, step in ((gl, gpg, gg, gsg), (ul, upg, ug, usg)):
            full[...] = dot(xt, pg[...])
            latent(sl, full, grad, step)


def specs(T, tile, rows, ff, early):
    a = (lambda i: jnp.minimum(i, T - 1)) if early else (lambda i: jnp.maximum(i - T, 0))
    b = (lambda i: jnp.maximum(i - T, 0)) if early else (lambda i: jnp.minimum(i, T - 1))
    return {
        "tok": pl.BlockSpec((rows, tile), lambda i: (0, a(i))),
        "wide": pl.BlockSpec((tile, ff), lambda i: (a(i), 0)),
        "wide_step": pl.BlockSpec((tile // GROUP, ff), lambda i: (a(i), 0)),
        "down": pl.BlockSpec((ff, tile), lambda i: (0, b(i))),
        "down_step": pl.BlockSpec((ff // GROUP, tile), lambda i: (0, b(i))),
        "rows": pl.BlockSpec((rows, tile), lambda i: (0, b(i))),
        "whole": pl.BlockSpec((rows, ff), lambda i: (0, 0)),
    }


def body(tokens, gate_weight, up_weight, down_weight, gate_step, up_step, down_step, *, count):
    D, ff = gate_weight.shape
    tile = 512
    T = D // tile
    Z, Y = split_axis(count)
    part = tokens.shape[0]
    rows = part * count
    shape = jax.ShapeDtypeStruct
    vmem = pl.BlockSpec(memory_space=pltpu.VMEM)
    hbm = pl.BlockSpec(memory_space=pl.ANY)
    whole, error, gate_pre, up_pre, hidden, slope_g, slope_u, slope_d, fake_d = pl.pallas_call(
        functools.partial(front_kernel, Z, Y, T),
        in_specs=[vmem, hbm, hbm, hbm, vmem, vmem, vmem],
        out_specs=[vmem] * 5 + [hbm] * 4,
        out_shape=[
            shape((Z, Y, 2, part, D), BF16), shape((Z, Y, 2, part, D), BF16),
            shape((rows, ff), F32), shape((rows, ff), F32), shape((rows, ff), BF16),
            shape((D, ff), BF16), shape((D, ff), BF16), shape((ff, D), BF16), shape((ff, D), BF16),
        ],
        scratch_shapes=[
            pltpu.VMEM((T, tile, ff), BF16), pltpu.VMEM((T, tile, ff), BF16),
            pltpu.VMEM((T, ff, tile), BF16),
            pltpu.VMEM((T, tile, ff), BF16), pltpu.VMEM((T, tile, ff), BF16),
            pltpu.VMEM((T, ff, tile), BF16),
            pltpu.VMEM((D // GROUP, ff), F32), pltpu.VMEM((D // GROUP, ff), F32),
            pltpu.VMEM((T, ff // GROUP, tile), F32),
            pltpu.VMEM((T, rows, tile), BF16),
            pltpu.VMEM((rows, ff), F32), pltpu.VMEM((rows, ff), F32), pltpu.VMEM((rows, ff), BF16),
            pltpu.VMEM((Z, Y, 2, part, D), BF16),
            pltpu.VMEM((Z, Y, part, D), BF16),
            pltpu.VMEM((Z, part, D), BF16),
            pltpu.VMEM((Z, part, D), F32),
            pltpu.VMEM((Z, part, D), BF16),
            pltpu.VMEM((Z - 1, part, D), BF16),
            pltpu.VMEM((Z - 1, part, D), BF16),
            pltpu.SemaphoreType.DMA((3, T)),
            pltpu.SemaphoreType.DMA((4, T)),
            pltpu.SemaphoreType.DMA((CHUNKS, Z + 1)),
            pltpu.SemaphoreType.DMA((CHUNKS, Z + 1)),
            pltpu.SemaphoreType.DMA((CHUNKS, 2 * Z + 2)),
            pltpu.SemaphoreType.DMA((CHUNKS, 2 * Z + 2)),
        ],
        compiler_params=pltpu.CompilerParams(
            collective_id=0, has_side_effects=True, vmem_limit_bytes=60 * 1024 * 1024
        ),
        name="front",
    )(tokens, gate_weight, up_weight, down_weight, gate_step, up_step, down_step)
    whole = whole.reshape(rows, D)
    error = error.reshape(rows, D)
    tile = 1024
    T = D // tile
    b = specs(T, tile, rows, ff, False)
    return tuple(pl.pallas_call(
        functools.partial(backward_kernel, T),
        grid=(2 * T,),
        in_specs=[b["rows"], b["tok"], b["whole"], b["whole"], b["whole"],
                  b["wide"], b["wide"], b["down"], b["down"]],
        out_specs=[b["wide"], b["wide"], b["down"],
                   b["wide_step"], b["wide_step"], b["down_step"]],
        out_shape=[shape((D, ff), BF16), shape((D, ff), BF16), shape((ff, D), BF16),
                   shape(gate_step.shape, F32), shape(up_step.shape, F32),
                   shape(down_step.shape, F32)],
        scratch_shapes=[
            pltpu.VMEM((ff, rows), BF16), pltpu.VMEM((rows, ff), F32),
            pltpu.VMEM((rows, ff), BF16), pltpu.VMEM((rows, ff), BF16),
            pltpu.VMEM((tile, ff), F32), pltpu.VMEM((ff, tile), F32),
        ],
        compiler_params=pltpu.CompilerParams(
            dimension_semantics=("arbitrary",), vmem_limit_bytes=VMEM_LIMIT
        ),
        name="backward",
    )(error, whole, hidden, gate_pre, up_pre, slope_g, slope_u, slope_d, fake_d))


def solution(mesh):
    return jax.shard_map(
        functools.partial(body, count=mesh.shape["tensor"]),
        mesh=mesh,
        in_specs=(
            P(("groups", "tensor"), None),
            P("groups", "tensor"),
            P("groups", "tensor"),
            P(("groups", "tensor"), None),
            P("groups", "tensor"),
            P("groups", "tensor"),
            P(("groups", "tensor"), None),
        ),
        out_specs=(
            P("groups", "tensor"),
            P("groups", "tensor"),
            P(("groups", "tensor"), None),
            P("groups", "tensor"),
            P("groups", "tensor"),
            P(("groups", "tensor"), None),
        ),
        check_vma=False,
    )
```
